128 devices in a mesh: row: 4 (over y), col: 16 (over x, z_hi, core), depth: 2 (over z_lo).
Axes of the slice: x: 4, y: 4, z: 4 (z_hi: 2, z_lo: 2; z = z_hi * 2 + z_lo), core: 2. Of those that a mesh axis runs over, the one named last changes fastest.
Arguments:
- values: bfloat16 [800, 80, 128, 128], P(('row', 'depth'), 'col'), may hold values from -2 to 2
- pattern: int32 [800, 80], P(('row', 'depth'), 'col'), may hold values from 0 to 49, as said below
- branch_flag: int32 [40], replicated, may hold values from 0 to 1, as said below
Outputs:
- purified: bfloat16 [40, 80, 128, 128], P(('row', 'depth'), 'col')
The draws below stay inside these ranges and needn't reach their ends.
Inputs may be any that keep to these rules, and one draw needn't show every extreme that they name: `pattern`: block columns fall into classes with 5 members in every column panel; block (i, j) is nonzero exactly when i and j are in the same class, and the 5 slots of a block row in panel c list, in no particular order, the distinct panel-local indices of the members of its class in that panel. `branch_flag`: exactly half of the entries, rounded down, are 1; the rest are 0.
All inputs are finite; a program needn't handle non-finite values.
Results may differ from the reference program's by a relative error of at most 0.001.
Values may be sent and summed in bfloat16 or wider, within the bound.
A program may use at most 128 MiB of HBM per device.

```python
import jax
import jax.numpy as jnp
from jax import lax

NB = 800
BS = 128
WL = 5
PANELS = 16
PANEL_COLS = 50
SLAB = 40
STRIDE = 20
N_COL = 16


def draw_pattern(key, part):
    panel_cols = NB // N_COL
    classes = panel_cols // WL
    subkeys = jax.random.split(jax.random.fold_in(key, 7), N_COL)

    def shuffle(subkey):
        return jax.random.permutation(subkey, panel_cols).astype(jnp.int32)
    orders = jax.vmap(shuffle)(subkeys)
    inverse = jnp.argsort(orders, axis=1).astype(jnp.int32)
    labels = (orders % classes).reshape(NB)
    wanted = labels[:, None, None] + classes * jnp.arange(WL, dtype=jnp.int32)[None, None, :]
    panel_index = jnp.arange(N_COL, dtype=jnp.int32)[None, :, None]
    picked = inverse[panel_index, wanted]
    return picked.reshape(NB, N_COL * WL).astype(jnp.int32)


def draw_branch_flag(key, part):
    order = jax.random.permutation(jax.random.fold_in(key, 11), SLAB).astype(jnp.int32)
    return (order % 2).astype(jnp.int32)


def level_of(stream_key, shape, cuts, low, top_value):
    gain, own = 1.0, jax.random.fold_in(stream_key, 6)
    for axis_at, blocks in cuts:
        heights = jnp.exp(jax.random.uniform(jax.random.fold_in(own, axis_at), (blocks,), jnp.float32, low / len(cuts), top_value / len(cuts)))
        gain = gain * jnp.repeat(heights, shape[axis_at] // blocks).reshape([-1 if axis == axis_at else 1 for axis in range(len(shape))])
    return gain


def bell_draw(stream_key, extent, scale, bound, pieces=(), kind=jnp.bfloat16):
    factor_of = level_of(stream_key, extent, pieces, -0.22, 0.18) if pieces else 1.0
    drawn = jax.random.normal(stream_key, extent, jnp.float32) * scale * factor_of
    return jnp.minimum(jnp.maximum(drawn, -bound), bound).astype(kind)


def setup_inputs(seed: int = 0) -> dict:
    streams_of = jax.random.split(jax.random.key(seed), 4)
    values = bell_draw(streams_of[0], (NB, PANELS * WL, BS, BS), 0.125, 2.0, ((0, 8), (1, 16)))
    pattern = draw_pattern(jax.random.fold_in(streams_of[3], 71), 0)
    branch_flag = draw_branch_flag(jax.random.fold_in(streams_of[3], 71), 0)
    return {"values": values, "pattern": pattern, "branch_flag": branch_flag}


def reference(values, pattern, branch_flag):
    slot_total = PANELS * WL
    panel_of = (jnp.arange(slot_total, dtype=jnp.int32) // WL).astype(jnp.int32)
    slab_rows = (jnp.arange(SLAB, dtype=jnp.int32) * STRIDE).astype(jnp.int32)

    def one_row(items):
        row_index, flag = items
        columns = pattern[row_index]
        inner = (panel_of * PANEL_COLS + columns).astype(jnp.int32)
        right = pattern[inner].reshape(slot_total, PANELS, WL)
        target = columns.reshape(PANELS, WL)
        match = right[:, :, None, :] == target[None, :, :, None]
        present = jnp.any(match, axis=3)
        slot_iota = lax.broadcasted_iota(jnp.int32, match.shape, 3)
        chosen = jnp.sum(jnp.where(match, slot_iota, 0), axis=3).astype(jnp.int32)
        panel_iota = lax.broadcasted_iota(jnp.int32, chosen.shape, 1)
        slot_index = (panel_iota * WL + chosen).reshape(slot_total, slot_total).astype(jnp.int32)
        picked = values[inner[:, None], slot_index]
        picked = jnp.where(present.reshape(slot_total, slot_total)[:, :, None, None], picked, jnp.zeros((), picked.dtype))
        left = values[row_index]
        square = jnp.einsum('lab,lqbc->qac', left.astype(jnp.float32), picked.astype(jnp.float32))
        own = values[row_index].astype(jnp.float32)
        result = jnp.where(flag == 1, square, 2.0 * own - square)
        return result.astype(jnp.bfloat16)

    return lax.map(one_row, (slab_rows, branch_flag))
```

```python
import functools

import jax
import jax.numpy as jnp
from jax import lax
from jax.experimental import pallas as pl
from jax.experimental.pallas import tpu as pltpu
from jax.sharding import PartitionSpec as P

W = 5
B = 128
WL = 5
R = WL * B
PR = R + 16
MESH = pl.DeviceIdType.MESH
F32 = jnp.float32
BF16 = jnp.bfloat16
TOP = 32512.0
STEPS = 128.0


def encode(dst, p):
    amax = jnp.max(jnp.abs(p), axis=0, keepdims=True)
    e = jnp.ceil(jnp.log2(jnp.maximum(amax, 1e-30)) * STEPS)
    q = jnp.round(p * (jnp.exp2(e * (-1.0 / STEPS)) * TOP)).astype(jnp.int32).astype(jnp.int16)
    for m in range(WL):
        dst[m * B : (m + 1) * B, :] = q[:, m * B : (m + 1) * B]
    e = e.astype(jnp.int32)
    rows = [e[:, m * B : (m + 1) * B] for m in range(WL)] + [jnp.zeros((16 - WL, B), jnp.int32)]
    dst[R:PR, :] = jnp.concatenate(rows, axis=0).astype(jnp.int16)


def decode(src):
    e = src[R:PR, :].astype(jnp.int32).astype(F32)
    scale = jnp.exp2(e * (1.0 / STEPS)) * (1.0 / TOP)
    parts = []
    for m in range(WL):
        q = src[m * B : (m + 1) * B, :].astype(jnp.int32).astype(F32)
        parts.append(q * scale[m : m + 1, :])
    return jnp.concatenate(parts, axis=1)


def kernel(
    flag_ref, vals, pat, out,
    rbuf, sbuf, lbuf, psend, precv, ctile, crecv, ktile, krecv, acc, idxv, idxs,
    ld_sem, r_sem, t_send, l_send, l_recv, p_send, p_recv, c_send, c_recv, k_send, k_recv, i_sem,
):
    y = lax.axis_index("row")
    zl = lax.axis_index("depth")
    col = lax.axis_index("col")
    x = col // 4
    zh = (col // 2) % 2
    core = col % 2
    g = y * 2 + zl

    def dev(dx, dy, dzh, dzl, dcore):
        return {"row": dy, "col": dx * 4 + dzh * 2 + dcore, "depth": dzl}

    xp, xm = (x + 1) % 4, (x + 3) % 4
    sib = dev(x, y, zh, zl, 1 - core)
    zx = dev(x, y, 1 - zh, zl, core)
    xpd, xmd = dev(xp, y, zh, zl, core), dev(xm, y, zh, zl, core)
    t_to = dev((x + y) % 4, x, zl, zh, core)
    t_from = dev(y, (x + 4 - y) % 4, zl, zh, core)
    away = jnp.logical_or(jnp.logical_or((x + y) % 4 != x, x != y), zl != zh)

    def source(cx, czh):
        return ((cx + 4 - y) % 4) * 2 + czh

    def group_dev(t):
        return dev(x, t // 2, zh, t % 2, core)

    def own_copy(w):
        return pltpu.make_async_copy(vals.at[pl.ds(20 * w * WL, WL)], sbuf.at[w], ld_sem.at[w])

    r_copy = pltpu.make_async_copy(vals, rbuf, r_sem)

    barrier = pltpu.get_barrier_semaphore()

    def greet(d):
        pl.semaphore_signal(barrier, inc=1, device_id=d, device_id_type=MESH)

    for d in (sib, zx, xpd, xmd):
        greet(d)
    for o in range(1, 8):
        greet(group_dev((g + o) % 8))

    @pl.when(away)
    def _():
        greet(t_to)
        greet(t_from)

    lane = lax.broadcasted_iota(jnp.int32, (1, B), 1)
    mine = jnp.logical_and(lane >= g * 16, lane < g * 16 + 16)
    ctile[...] = jnp.zeros((W, 8, B), jnp.int32)
    ktile[0] = jnp.zeros((8, B), jnp.int32)
    for w in range(W):
        krow = jnp.zeros((1, B), jnp.int32)
        for s in range(WL):
            v = jnp.broadcast_to(pat[20 * w : 20 * w + 1, s : s + 1], (1, B))
            ctile[w, s : s + 1, :] = jnp.where(mine, v, 0)
            krow = jnp.where(lane == g * 16 + core * WL + s, v + core * 50, krow)
        ktile[0, w : w + 1, :] = krow

    @pl.when(away)
    def _():
        pl.semaphore_wait(barrier, 13)

    @pl.when(jnp.logical_not(away))
    def _():
        pl.semaphore_wait(barrier, 11)

    def remote(src, dst, ssem, rsem, d):
        return pltpu.make_async_remote_copy(
            src_ref=src, dst_ref=dst, send_sem=ssem, recv_sem=rsem, device_id=d, device_id_type=MESH
        )

    def t_copy(w):
        return remote(
            vals.at[pl.ds(20 * w * WL, WL)], lbuf.at[w, g, core], t_send.at[w], l_recv.at[w, g, core], t_to
        )

    def t_start(w):
        @pl.when(away)
        def _():
            t_copy(w).start()

        @pl.when(jnp.logical_not(away))
        def _():
            pltpu.make_async_copy(
                vals.at[pl.ds(20 * w * WL, WL)], lbuf.at[w, g, core], l_recv.at[w, g, core]
            ).start()

    def k_copy(src, k, d):
        return remote(src, krecv.at[k], k_send.at[k], k_recv.at[k], d)

    def k_start():
        @pl.when(away)
        def _():
            k_copy(ktile.at[0], 0, t_to).start()

        @pl.when(jnp.logical_not(away))
        def _():
            pltpu.make_async_copy(ktile.at[0], krecv.at[0], k_recv.at[0]).start()

    def k_got(k):
        k_copy(ktile.at[0], k, sib).wait_recv()

    def c_copy(o):
        return remote(ctile, crecv.at[g], c_send.at[o - 1], c_recv.at[g], group_dev((g + o) % 8))

    def piece_copy(w, gs, d, k):
        slot = lbuf.at[w, gs, core]
        return remote(slot, slot, l_send.at[w, k], l_recv.at[w, gs, core], d)

    def got(w, gs, p):
        slot = lbuf.at[w, gs, p]
        remote(slot, slot, l_send.at[w, 0], l_recv.at[w, gs, p], sib).wait_recv()

    own = source(x, zh)
    ownz = source(x, 1 - zh)
    left = source(xm, zh)
    leftz = source(xm, 1 - zh)
    right = source(xp, zh)
    rightz = source(xp, 1 - zh)
    far0 = source((x + 2) % 4, 0)
    far1 = source((x + 2) % 4, 1)
    sends = (
        (own, zx), (own, xpd), (own, xmd), (own, sib),
        (ownz, xpd), (ownz, xmd), (ownz, sib),
        (source(xm, 0), xpd), (source(xp, 1), xmd),
        (left, sib), (leftz, sib), (right, sib), (rightz, sib),
        (far0, sib), (far1, sib),
    )

    def send(w, *numbers):
        for k in numbers:
            piece_copy(w, sends[k][0], sends[k][1], k).start()

    def relay_a(w):
        got(w, own, core)
        send(w, 0, 1, 2, 3)

    def relay_b(w):
        got(w, ownz, core)
        send(w, 4, 5, 6)

    def relay_c(w):
        for gs in (left, right, leftz, rightz):
            got(w, gs, core)
        send(w, 7, 8, 9, 10, 11, 12)

    def relay_d(w):
        got(w, far0, core)
        got(w, far1, core)
        send(w, 13, 14)

    def relay_e(w):
        for gs in range(8):
            got(w, gs, 1 - core)

    def make_index():
        total = ktile[2] + krecv[3] + krecv[4] + krecv[5]
        rows = lax.broadcasted_iota(jnp.int32, (100, B), 0)
        slots = [jnp.broadcast_to(pat[:, s : s + 1], (100, B)) for s in range(WL)]
        for w in range(W):
            kv = total[w : w + 1, :]
            here = rows == kv
            cols = ctile[w]
            for o in range(1, 8):
                cols = cols + crecv[(g + o) % 8, w]
            idx = jnp.broadcast_to(kv * WL, (8, B))
            for s in range(1, WL):
                right = jnp.sum(jnp.where(here, slots[s], 0), axis=0, keepdims=True)
                idx = idx + jnp.where(right == cols, s, 0)
            idxv[w] = idx
        copy = pltpu.make_async_copy(idxv, idxs, i_sem)
        copy.start()
        copy.wait()

    def product(w, gs):
        lc = jnp.concatenate(
            [lbuf[w, gs, p, s] for p in range(2) for s in range(WL)], axis=1
        )

        def block(m, l):
            return rbuf[idxs[w, m, gs * 16 + l]]

        rc = jnp.concatenate(
            [jnp.concatenate([block(m, l) for m in range(WL)], axis=1) for l in range(2 * WL)], axis=0
        )
        return jnp.dot(lc, rc, preferred_element_type=F32)

    def p_copy(w, k, d):
        return remote(psend.at[w, k], precv.at[w, k], p_send.at[w, k], p_recv.at[w, k], d)

    def y_dev(t):
        return dev(x, (y + 1 + 2 * t) % 4, zh, zl, core)

    zl_dev = dev(x, y, zh, 1 - zl, core)

    def pair(step):
        def body(t, carry):
            step(t)
            return carry

        lax.fori_loop(0, 2, body, 0)

    def far_rows(w):
        def step(t):
            encode(psend.at[w, t], product(w, ((y + 2) % 4) * 2 + t))
            p_copy(w, t, y_dev(t)).start()

        pair(step)

    def near_rows(w):
        def step(t):
            encode(psend.at[w, 2 + t], product(w, ((y + 1 + 2 * t) % 4) * 2 + 1 - t))
            p_copy(w, 2 + t, y_dev(t)).start()

        pair(step)

    def own_rows(w):
        def step(t):
            acc[w % 2, t] = product(w, y * 2 + t)

        pair(step)

    def joined_rows(w):
        def step(t):
            p = product(w, ((y + 1 + 2 * t) % 4) * 2 + t)
            p_copy(w, t, y_dev(t)).wait_recv()
            encode(psend.at[w, 4 + t], p + decode(precv.at[w, t]))
            p_copy(w, 4 + t, y_dev(t)).start()

        pair(step)

    def plane_sum(w, tz):
        a, b = 4 - 2 * tz, 3 + 2 * tz
        p_copy(w, b, zl_dev).wait_recv()
        p_copy(w, a, zl_dev).wait_recv()
        return acc[w % 2, tz] + decode(precv.at[w, a]) + decode(precv.at[w, b])

    def cross(w):
        encode(psend.at[w, 6], plane_sum(w, 1 - zl))
        p_copy(w, 6, zl_dev).start()

    def finish(w):
        own_copy(w).wait()
        s = plane_sum(w, zl)
        p_copy(w, 6, zl_dev).wait_recv()
        s = s + decode(precv.at[w, 6])
        plain = flag_ref[g * WL + w] == 1
        c_s = jnp.where(plain, 1.0, -1.0)
        c_o = jnp.where(plain, 0.0, 2.0)
        for m in range(WL):
            o = sbuf[w, m].astype(F32)
            out[w, m] = (
                c_s * s[:, m * B : (m + 1) * B] + c_o * o
            ).astype(BF16)

    t_start(0)
    k_start()
    t_start(1)
    for o in range(1, 8):
        c_copy(o).start()
    r_copy.start()
    k_got(0)
    k_copy(krecv.at[0], 1, sib).start()
    relay_a(0)
    t_start(2)
    k_got(1)
    ktile[1] = krecv[0] + krecv[1]
    k_copy(ktile.at[1], 2, zx).start()
    relay_b(0)
    t_start(3)
    relay_a(1)
    k_got(2)
    ktile[2] = ktile[1] + krecv[2]
    k_copy(ktile.at[2], 3, xpd).start()
    k_copy(ktile.at[2], 4, xmd).start()
    relay_b(1)
    relay_c(0)
    t_start(4)
    k_got(3)
    k_got(4)
    k_copy(krecv.at[3], 5, xpd).start()
    for w in range(W):
        own_copy(w).start()
    for o in range(1, 8):
        remote(
            ctile, crecv.at[(g + o) % 8], c_send.at[o - 1], c_recv.at[(g + o) % 8], sib
        ).wait_recv()
    relay_d(0)
    k_got(5)
    make_index()
    r_copy.wait()

    def wave(w, carry):
        def guard(cond, f, v):
            @pl.when(cond)
            def _():
                f(v)

        def first(v):
            relay_e(v)
            far_rows(v)

        guard(w < W, first, w)
        guard(w < W - 2, relay_a, w + 2)
        guard(w < W, near_rows, w)
        guard(w < W - 1, relay_c, w + 1)
        guard(w < W - 2, relay_b, w + 2)
        guard(w < W, own_rows, w)
        guard(w < W, joined_rows, w)
        guard(w < W - 1, relay_d, w + 1)
        return carry

    def wave_tail(w, carry):
        @pl.when(w > 0)
        def _():
            cross(w - 1)

        wave_body(w)

        @pl.when(w > 0)
        def _():
            finish(w - 1)

        return carry

    def wave_body(w):
        @pl.when(w < W)
        def _():
            wave(w, 0)

    lax.fori_loop(0, W + 1, wave_tail, 0)

    def drain(w, carry):
        @pl.when(away)
        def _():
            t_copy(w).wait_send()

        for k in range(15):
            piece_copy(w, sends[k][0], sends[k][1], k).wait_send()
        for k in range(7):
            p_copy(w, k, zl_dev).wait_send()
        return carry

    lax.fori_loop(0, W, drain, 0)
    for o in range(1, 8):
        c_copy(o).wait_send()

    @pl.when(away)
    def _():
        k_copy(ktile.at[0], 0, t_to).wait_send()

    for k in range(1, 6):
        k_copy(ktile.at[0], k, sib).wait_send()


def body(values, pattern, branch_flag):
    vmem = pl.BlockSpec(memory_space=pltpu.VMEM)
    dma = pltpu.SemaphoreType.DMA
    return pl.pallas_call(
        kernel,
        out_shape=jax.ShapeDtypeStruct((W, WL, B, B), BF16),
        in_specs=[pl.BlockSpec(memory_space=pltpu.SMEM), pl.BlockSpec(memory_space=pl.ANY), vmem],
        out_specs=vmem,
        scratch_shapes=[
            pltpu.VMEM((500, B, B), BF16),
            pltpu.VMEM((W, WL, B, B), BF16),
            pltpu.VMEM((W, 8, 2, WL, B, B), BF16),
            pltpu.VMEM((W, 7, PR, B), jnp.int16),
            pltpu.VMEM((W, 7, PR, B), jnp.int16),
            pltpu.VMEM((W, 8, B), jnp.int32),
            pltpu.VMEM((8, W, 8, B), jnp.int32),
            pltpu.VMEM((3, 8, B), jnp.int32),
            pltpu.VMEM((6, 8, B), jnp.int32),
            pltpu.VMEM((2, 2, B, R), F32),
            pltpu.VMEM((W, 8, B), jnp.int32),
            pltpu.SMEM((W, 8, B), jnp.int32),
            dma((W,)), dma, dma((W,)), dma((W, 15)), dma((W, 8, 2)), dma((W, 7)), dma((W, 7)),
            dma((7,)), dma((8,)), dma((6,)), dma((6,)), dma,
        ],
        compiler_params=pltpu.CompilerParams(
            collective_id=0, has_side_effects=True, vmem_limit_bytes=58 * 2**20
        ),
        cost_estimate=pl.CostEstimate(flops=8_400_000_000, bytes_accessed=20_000_000, transcendentals=0),
    )(branch_flag, values.reshape(500, B, B), pattern)


def solution(mesh):
    in_specs = (P(("row", "depth"), "col", None, None), P(("row", "depth"), "col"), P())
    out_specs = P(("row", "depth"), "col", None, None)
    return jax.shard_map(body, mesh=mesh, in_specs=in_specs, out_specs=out_specs, check_vma=False)
```

```python
import functools

import jax
import jax.numpy as jnp
from jax import lax
from jax.experimental import pallas as pl
from jax.experimental.pallas import tpu as pltpu
from jax.sharding import PartitionSpec as P

W = 5
B = 128
WL = 5
R = WL * B
PR = R + 16
MESH = pl.DeviceIdType.MESH
F32 = jnp.float32
BF16 = jnp.bfloat16
TOP = 32512.0
STEPS = 128.0


def encode(dst, p):
    amax = jnp.max(jnp.abs(p), axis=0, keepdims=True)
    e = jnp.ceil(jnp.log2(jnp.maximum(amax, 1e-30)) * STEPS)
    q = jnp.round(p * (jnp.exp2(e * (-1.0 / STEPS)) * TOP)).astype(jnp.int32).astype(jnp.int16)
    for m in range(WL):
        dst[m * B : (m + 1) * B, :] = q[:, m * B : (m + 1) * B]
    e = e.astype(jnp.int32)
    rows = [e[:, m * B : (m + 1) * B] for m in range(WL)] + [jnp.zeros((16 - WL, B), jnp.int32)]
    dst[R:PR, :] = jnp.concatenate(rows, axis=0).astype(jnp.int16)


def decode(src):
    e = src[R:PR, :].astype(jnp.int32).astype(F32)
    scale = jnp.exp2(e * (1.0 / STEPS)) * (1.0 / TOP)
    parts = []
    for m in range(WL):
        q = src[m * B : (m + 1) * B, :].astype(jnp.int32).astype(F32)
        parts.append(q * scale[m : m + 1, :])
    return jnp.concatenate(parts, axis=1)


def kernel(
    flag_ref, vals, pat, out,
    rbuf, sbuf, lbuf, psend, precv, ctile, crecv, ktile, krecv, acc, idxv, idxs,
    ld_sem, r_sem, t_send, l_send, l_recv, p_send, p_recv, c_send, c_recv, k_send, k_recv, i_sem,
):
    y = lax.axis_index("row")
    zl = lax.axis_index("depth")
    col = lax.axis_index("col")
    x = col // 4
    zh = (col // 2) % 2
    core = col % 2
    g = y * 2 + zl

    def spread(a, b, p):
        a, b = a * (1 + 2 * p) % 4, b * (1 + 2 * p) % 4
        a1, a0, b1, b0 = a // 2, a % 2, b // 2, b % 2
        return (((a0 + a1 + b0) % 2) * 2 + (a1 + b0 + b1) % 2) * (1 + 2 * p) % 4

    def dev(dx, dy, dzh, dzl, dcore):
        return {"row": dy, "col": dx * 4 + dzh * 2 + dcore, "depth": dzl}

    xp, xm = (x + 1) % 4, (x + 3) % 4
    sib = dev(x, y, zh, zl, 1 - core)
    zx = dev(x, y, 1 - zh, zl, core)
    xpd, xmd = dev(xp, y, zh, zl, core), dev(xm, y, zh, zl, core)
    to_x = spread(x, y, core)
    t_to = dev(to_x, x, zl, zh, core)
    t_from = dev(y, to_x, zl, zh, core)
    away = jnp.logical_or(x != y, zl != zh)

    def place(gs, p):
        return spread(y, gs // 2, p) * 2 + gs % 2

    def group_dev(t):
        return dev(x, t // 2, zh, t % 2, core)

    def own_copy(w):
        return pltpu.make_async_copy(vals.at[pl.ds(20 * w * WL, WL)], sbuf.at[w], ld_sem.at[w])

    r_copy = pltpu.make_async_copy(vals, rbuf, r_sem)

    barrier = pltpu.get_barrier_semaphore()

    def greet(d):
        pl.semaphore_signal(barrier, inc=1, device_id=d, device_id_type=MESH)

    for d in (sib, zx, xpd, xmd):
        greet(d)
    for o in range(1, 8):
        greet(group_dev((g + o) % 8))

    @pl.when(away)
    def _():
        greet(t_to)
        greet(t_from)

    lane = lax.broadcasted_iota(jnp.int32, (1, B), 1)
    ctile[...] = jnp.zeros((8, B), jnp.int32)
    ktile[0] = jnp.zeros((8, B), jnp.int32)
    for w in range(W):
        crow = jnp.zeros((1, B), jnp.int32)
        krow = jnp.zeros((1, B), jnp.int32)
        for s in range(WL):
            v = jnp.broadcast_to(pat[20 * w : 20 * w + 1, s : s + 1], (1, B))
            crow = jnp.where(lane == s, v, crow)
            krow = jnp.where(lane == g * 16 + core * WL + s, v + core * 50, krow)
        ctile[w : w + 1, :] = crow
        ktile[0, w : w + 1, :] = krow

    @pl.when(away)
    def _():
        pl.semaphore_wait(barrier, 13)

    @pl.when(jnp.logical_not(away))
    def _():
        pl.semaphore_wait(barrier, 11)

    def remote(src, dst, ssem, rsem, d):
        return pltpu.make_async_remote_copy(
            src_ref=src, dst_ref=dst, send_sem=ssem, recv_sem=rsem, device_id=d, device_id_type=MESH
        )

    def t_copy(w):
        return remote(
            vals.at[pl.ds(20 * w * WL, WL)],
            lbuf.at[w, to_x * 2 + zl, core],
            t_send.at[w],
            l_recv.at[w, to_x * 2 + zl, core],
            t_to,
        )

    def t_start(w):
        @pl.when(away)
        def _():
            t_copy(w).start()

        @pl.when(jnp.logical_not(away))
        def _():
            slot = x * 2 + zl
            pltpu.make_async_copy(
                vals.at[pl.ds(20 * w * WL, WL)], lbuf.at[w, slot, core], l_recv.at[w, slot, core]
            ).start()

    def k_copy(src, k, d):
        return remote(src, krecv.at[k], k_send.at[k], k_recv.at[k], d)

    def k_start():
        @pl.when(away)
        def _():
            k_copy(ktile.at[0], 0, t_to).start()

        @pl.when(jnp.logical_not(away))
        def _():
            pltpu.make_async_copy(ktile.at[0], krecv.at[0], k_recv.at[0]).start()

    def k_got(k):
        k_copy(ktile.at[0], k, sib).wait_recv()

    def c_copy(o):
        return remote(ctile, crecv.at[g], c_send.at[o - 1], c_recv.at[g], group_dev((g + o) % 8))

    def got(w, q, p):
        slot = lbuf.at[w, q, p]
        remote(slot, slot, l_send.at[w, 0], l_recv.at[w, q, p], sib).wait_recv()

    on_x, back_x = (x + 1 + 2 * core) % 4, (x + 3 + 2 * core) % 4
    on, back = dev(on_x, y, zh, zl, core), dev(back_x, y, zh, zl, core)
    q = {
        "own": x * 2 + zh, "own_z": x * 2 + 1 - zh,
        "ahead": on_x * 2 + zh, "ahead_z": on_x * 2 + 1 - zh,
        "behind": back_x * 2 + zh, "behind_z": back_x * 2 + 1 - zh,
        "far": (x + 2) % 4 * 2 + zh, "far_z": (x + 2) % 4 * 2 + 1 - zh,
    }
    sends = (
        ("own", on), ("own", back), ("own", zx), ("own", sib),
        ("own_z", on), ("own_z", sib),
        ("ahead", back), ("behind_z", on), ("ahead", zx),
        ("behind", sib), ("ahead", sib), ("behind_z", sib),
        ("far", sib), ("far_z", sib), ("ahead_z", sib),
    )

    def piece_copy(w, k):
        slot = lbuf.at[w, q[sends[k][0]], core]
        return remote(slot, slot, l_send.at[w, k], l_recv.at[w, q[sends[k][0]], core], sends[k][1])

    def relay(w, arrived, numbers):
        for name in arrived:
            got(w, q[name], core)
        for k in numbers:
            piece_copy(w, k).start()

    def relay_a(w):
        relay(w, ("own",), (0, 1, 2, 3))

    def relay_b(w):
        relay(w, ("own_z",), (4, 5))

    def relay_c(w):
        relay(w, ("ahead", "behind", "behind_z"), (6, 7, 8, 9, 10, 11))

    def relay_d(w):
        relay(w, ("far", "far_z", "ahead_z"), (12, 13, 14))

    def relay_e(w):
        for i in range(8):
            got(w, i, 1 - core)

    def make_index():
        total = ktile[2] + krecv[3] + krecv[4] + krecv[5]
        rows = lax.broadcasted_iota(jnp.int32, (100, B), 0)
        owner = lax.broadcasted_iota(jnp.int32, (8, B), 1) // 16
        crecv[g] = ctile[...]
        rights = []
        for s in range(1, WL):
            slots = jnp.broadcast_to(pat[:, s : s + 1], (100, B))
            parts = [
                jnp.sum(jnp.where(rows == total[w : w + 1, :], slots, 0), axis=0, keepdims=True)
                for w in range(W)
            ]
            rights.append(jnp.concatenate(parts + [jnp.zeros((8 - W, B), jnp.int32)], axis=0))
        for m in range(WL):
            cols = jnp.zeros((8, B), jnp.int32)
            for t in range(8):
                cols = jnp.where(owner == t, jnp.broadcast_to(crecv[t, :, m : m + 1], (8, B)), cols)
            idx = total * WL
            for s in range(1, WL):
                idx = idx + jnp.where(rights[s - 1] == cols, s, 0)
            idxv[m] = idx
        copy = pltpu.make_async_copy(idxv, idxs, i_sem)
        copy.start()
        copy.wait()

    def product(w, gs):
        at = [place(gs, p) for p in range(2)]
        lc = jnp.concatenate(
            [lbuf[w, at[p], p, s] for p in range(2) for s in range(WL)], axis=1
        )

        def block(m, l):
            return rbuf[idxs[m, w, gs * 16 + l]]

        rc = jnp.concatenate(
            [jnp.concatenate([block(m, l) for m in range(WL)], axis=1) for l in range(2 * WL)], axis=0
        )
        return jnp.dot(lc, rc, preferred_element_type=F32)

    def p_copy(w, k, d):
        return remote(psend.at[w, k], precv.at[w, k], p_send.at[w, k], p_recv.at[w, k], d)

    def y_dev(t):
        return dev(x, (y + 1 + 2 * t) % 4, zh, zl, core)

    zl_dev = dev(x, y, zh, 1 - zl, core)

    def pair(step):
        def body(t, carry):
            step(t)
            return carry

        lax.fori_loop(0, 2, body, 0)

    def far_rows(w):
        def step(t):
            encode(psend.at[w, t], product(w, ((y + 2) % 4) * 2 + t))
            p_copy(w, t, y_dev(t)).start()

        pair(step)

    def near_rows(w):
        def step(t):
            encode(psend.at[w, 2 + t], product(w, ((y + 1 + 2 * t) % 4) * 2 + 1 - t))
            p_copy(w, 2 + t, y_dev(t)).start()

        pair(step)

    def own_rows(w):
        def step(t):
            acc[w % 3, t] = product(w, y * 2 + t)

        pair(step)

    def joined_rows(w):
        def step(t):
            p = product(w, ((y + 1 + 2 * t) % 4) * 2 + t)
            p_copy(w, t, y_dev(t)).wait_recv()
            encode(psend.at[w, 4 + t], p + decode(precv.at[w, t]))
            p_copy(w, 4 + t, y_dev(t)).start()

        pair(step)

    def plane_sum(w, tz):
        a, b = 4 - 2 * tz, 3 + 2 * tz
        p_copy(w, b, zl_dev).wait_recv()
        p_copy(w, a, zl_dev).wait_recv()
        return acc[w % 3, tz] + decode(precv.at[w, a]) + decode(precv.at[w, b])

    def cross(w):
        encode(psend.at[w, 6], plane_sum(w, 1 - zl))
        p_copy(w, 6, zl_dev).start()

    def finish(w):
        own_copy(w).wait()
        s = plane_sum(w, zl)
        p_copy(w, 6, zl_dev).wait_recv()
        s = s + decode(precv.at[w, 6])
        plain = flag_ref[g * WL + w] == 1
        c_s = jnp.where(plain, 1.0, -1.0)
        c_o = jnp.where(plain, 0.0, 2.0)
        for m in range(WL):
            o = sbuf[w, m].astype(F32)
            out[w, m] = (
                c_s * s[:, m * B : (m + 1) * B] + c_o * o
            ).astype(BF16)

    k_start()
    t_start(0)
    t_start(1)
    for o in range(1, 8):
        c_copy(o).start()
    r_copy.start()
    k_got(0)
    k_copy(krecv.at[0], 1, sib).start()
    relay_a(0)
    t_start(2)
    k_got(1)
    ktile[1] = krecv[0] + krecv[1]
    k_copy(ktile.at[1], 2, zx).start()
    relay_a(1)
    relay_b(0)
    k_got(2)
    ktile[2] = ktile[1] + krecv[2]
    k_copy(ktile.at[2], 3, xpd).start()
    k_copy(ktile.at[2], 4, xmd).start()
    t_start(3)
    relay_c(0)
    k_got(3)
    k_got(4)
    k_copy(krecv.at[3], 5, xpd).start()
    relay_b(1)
    t_start(4)
    relay_a(2)
    for w in range(W):
        own_copy(w).start()
    for o in range(1, 8):
        remote(
            ctile, crecv.at[(g + o) % 8], c_send.at[o - 1], c_recv.at[(g + o) % 8], sib
        ).wait_recv()
    k_got(5)
    relay_d(0)
    make_index()
    relay_b(2)
    r_copy.wait()

    def wave(w, carry):
        def guard(cond, f, v):
            @pl.when(cond)
            def _():
                f(v)

        def first(v):
            relay_e(v)
            far_rows(v)

        guard(w < W, first, w)
        guard(w < W - 1, relay_c, w + 1)
        guard(w < W, near_rows, w)
        guard(w < W, own_rows, w)
        guard(w < W - 3, relay_a, w + 3)
        guard(w < W - 3, relay_b, w + 3)
        guard(w < W - 1, relay_d, w + 1)
        guard(jnp.logical_and(w > 0, w < W + 1), cross, w - 1)
        guard(w < W, joined_rows, w)
        guard(w > 1, finish, w - 2)
        return carry

    lax.fori_loop(0, W + 2, wave, 0)

    def drain(w, carry):
        @pl.when(away)
        def _():
            t_copy(w).wait_send()

        for k in range(15):
            piece_copy(w, k).wait_send()
        for k in range(7):
            p_copy(w, k, zl_dev).wait_send()
        return carry

    lax.fori_loop(0, W, drain, 0)
    for o in range(1, 8):
        c_copy(o).wait_send()

    @pl.when(away)
    def _():
        k_copy(ktile.at[0], 0, t_to).wait_send()

    for k in range(1, 6):
        k_copy(ktile.at[0], k, sib).wait_send()


def body(values, pattern, branch_flag):
    vmem = pl.BlockSpec(memory_space=pltpu.VMEM)
    dma = pltpu.SemaphoreType.DMA
    return pl.pallas_call(
        kernel,
        out_shape=jax.ShapeDtypeStruct((W, WL, B, B), BF16),
        in_specs=[pl.BlockSpec(memory_space=pltpu.SMEM), pl.BlockSpec(memory_space=pl.ANY), vmem],
        out_specs=vmem,
        scratch_shapes=[
            pltpu.VMEM((500, B, B), BF16),
            pltpu.VMEM((W, WL, B, B), BF16),
            pltpu.VMEM((W, 8, 2, WL, B, B), BF16),
            pltpu.VMEM((W, 7, PR, B), jnp.int16),
            pltpu.VMEM((W, 7, PR, B), jnp.int16),
            pltpu.VMEM((8, B), jnp.int32),
            pltpu.VMEM((8, 8, B), jnp.int32),
            pltpu.VMEM((3, 8, B), jnp.int32),
            pltpu.VMEM((6, 8, B), jnp.int32),
            pltpu.VMEM((3, 2, B, R), F32),
            pltpu.VMEM((WL, 8, B), jnp.int32),
            pltpu.SMEM((WL, 8, B), jnp.int32),
            dma((W,)), dma, dma((W,)), dma((W, 15)), dma((W, 8, 2)), dma((W, 7)), dma((W, 7)),
            dma((7,)), dma((8,)), dma((6,)), dma((6,)), dma,
        ],
        compiler_params=pltpu.CompilerParams(
            collective_id=0, has_side_effects=True, vmem_limit_bytes=58 * 2**20
        ),
        cost_estimate=pl.CostEstimate(flops=8_400_000_000, bytes_accessed=20_000_000, transcendentals=0),
    )(branch_flag, values.reshape(500, B, B), pattern)


def solution(mesh):
    in_specs = (P(("row", "depth"), "col", None, None), P(("row", "depth"), "col"), P())
    out_specs = P(("row", "depth"), "col", None, None)
    return jax.shard_map(body, mesh=mesh, in_specs=in_specs, out_specs=out_specs, check_vma=False)
```

```python
import functools

import jax
import jax.numpy as jnp
from jax import lax
from jax.experimental import pallas as pl
from jax.experimental.pallas import tpu as pltpu
from jax.sharding import PartitionSpec as P

W = 5
B = 128
WL = 5
R = WL * B
PR = R + 16
MESH = pl.DeviceIdType.MESH
F32 = jnp.float32
BF16 = jnp.bfloat16
TOP = 32512.0
STEPS = 128.0


def encode(dst, p):
    amax = jnp.max(jnp.abs(p), axis=0, keepdims=True)
    e = jnp.ceil(jnp.log2(jnp.maximum(amax, 1e-30)) * STEPS)
    q = jnp.round(p * (jnp.exp2(e * (-1.0 / STEPS)) * TOP)).astype(jnp.int32).astype(jnp.int16)
    for m in range(WL):
        dst[m * B : (m + 1) * B, :] = q[:, m * B : (m + 1) * B]
    e = e.astype(jnp.int32)
    rows = [e[:, m * B : (m + 1) * B] for m in range(WL)] + [jnp.zeros((16 - WL, B), jnp.int32)]
    dst[R:PR, :] = jnp.concatenate(rows, axis=0).astype(jnp.int16)


def decode(src):
    e = src[R:PR, :].astype(jnp.int32).astype(F32)
    scale = jnp.exp2(e * (1.0 / STEPS)) * (1.0 / TOP)
    parts = []
    for m in range(WL):
        q = src[m * B : (m + 1) * B, :].astype(jnp.int32).astype(F32)
        parts.append(q * scale[m : m + 1, :])
    return jnp.concatenate(parts, axis=1)


def kernel(
    flag_ref, vals, pat, out,
    rbuf, sbuf, lbuf, psend, precv, ctile, crecv, ktile, krecv, acc, idxv, idxs,
    ld_sem, r_sem, t_send, l_send, l_recv, p_send, p_recv, c_send, c_recv, k_send, k_recv, i_sem,
):
    y = lax.axis_index("row")
    zl = lax.axis_index("depth")
    col = lax.axis_index("col")
    x = col // 4
    zh = (col // 2) % 2
    core = col % 2
    g = y * 2 + zl

    def spread(a, b, p):
        a, b = a * (1 + 2 * p) % 4, b * (1 + 2 * p) % 4
        a1, a0, b1, b0 = a // 2, a % 2, b // 2, b % 2
        return (((a0 + a1 + b0) % 2) * 2 + (a1 + b0 + b1) % 2) * (1 + 2 * p) % 4

    def dev(dx, dy, dzh, dzl, dcore):
        return {"row": dy, "col": dx * 4 + dzh * 2 + dcore, "depth": dzl}

    xp, xm = (x + 1) % 4, (x + 3) % 4
    sib = dev(x, y, zh, zl, 1 - core)
    zx = dev(x, y, 1 - zh, zl, core)
    xpd, xmd = dev(xp, y, zh, zl, core), dev(xm, y, zh, zl, core)
    to_x = spread(x, y, core)
    t_to = dev(to_x, x, zl, zh, core)
    t_from = dev(y, to_x, zl, zh, core)
    away = jnp.logical_or(x != y, zl != zh)

    def place(gs, p):
        return spread(y, gs // 2, p) * 2 + gs % 2

    def group_dev(t):
        return dev(x, t // 2, zh, t % 2, core)

    def own_copy(w):
        return pltpu.make_async_copy(vals.at[pl.ds(20 * w * WL, WL)], sbuf.at[w], ld_sem.at[w])

    r_copy = pltpu.make_async_copy(vals, rbuf, r_sem)

    barrier = pltpu.get_barrier_semaphore()

    def greet(d):
        pl.semaphore_signal(barrier, inc=1, device_id=d, device_id_type=MESH)

    for d in (sib, zx, xpd, xmd):
        greet(d)
    for o in range(1, 8):
        greet(group_dev((g + o) % 8))

    @pl.when(away)
    def _():
        greet(t_to)
        greet(t_from)

    lane = lax.broadcasted_iota(jnp.int32, (1, B), 1)
    ctile[...] = jnp.zeros((8, B), jnp.int32)
    ktile[0] = jnp.zeros((8, B), jnp.int32)
    for w in range(W):
        crow = jnp.zeros((1, B), jnp.int32)
        krow = jnp.zeros((1, B), jnp.int32)
        for s in range(WL):
            v = jnp.broadcast_to(pat[20 * w : 20 * w + 1, s : s + 1], (1, B))
            crow = jnp.where(lane == s, v, crow)
            krow = jnp.where(lane == g * 16 + core * WL + s, v + core * 50, krow)
        ctile[w : w + 1, :] = crow
        ktile[0, w : w + 1, :] = krow

    @pl.when(away)
    def _():
        pl.semaphore_wait(barrier, 13)

    @pl.when(jnp.logical_not(away))
    def _():
        pl.semaphore_wait(barrier, 11)

    def remote(src, dst, ssem, rsem, d):
        return pltpu.make_async_remote_copy(
            src_ref=src, dst_ref=dst, send_sem=ssem, recv_sem=rsem, device_id=d, device_id_type=MESH
        )

    def t_copy(w):
        return remote(
            vals.at[pl.ds(20 * w * WL, WL)],
            lbuf.at[w, to_x * 2 + zl, core],
            t_send.at[w],
            l_recv.at[w, to_x * 2 + zl, core],
            t_to,
        )

    def t_start(w):
        @pl.when(away)
        def _():
            t_copy(w).start()

        @pl.when(jnp.logical_not(away))
        def _():
            slot = x * 2 + zl
            pltpu.make_async_copy(
                vals.at[pl.ds(20 * w * WL, WL)], lbuf.at[w, slot, core], l_recv.at[w, slot, core]
            ).start()

    def k_copy(src, k, d):
        return remote(src, krecv.at[k], k_send.at[k], k_recv.at[k], d)

    def k_start():
        @pl.when(away)
        def _():
            k_copy(ktile.at[0], 0, t_to).start()

        @pl.when(jnp.logical_not(away))
        def _():
            pltpu.make_async_copy(ktile.at[0], krecv.at[0], k_recv.at[0]).start()

    def k_got(k):
        k_copy(ktile.at[0], k, sib).wait_recv()

    def c_copy(o):
        return remote(ctile, crecv.at[g], c_send.at[o - 1], c_recv.at[g], group_dev((g + o) % 8))

    def got(w, q, p):
        slot = lbuf.at[w, q, p]
        remote(slot, slot, l_send.at[w, 0], l_recv.at[w, q, p], sib).wait_recv()

    on_x, back_x = (x + 1 + 2 * core) % 4, (x + 3 + 2 * core) % 4
    on, back = dev(on_x, y, zh, zl, core), dev(back_x, y, zh, zl, core)
    q = {
        "own": x * 2 + zh, "own_z": x * 2 + 1 - zh,
        "ahead": on_x * 2 + zh, "ahead_z": on_x * 2 + 1 - zh,
        "behind": back_x * 2 + zh, "behind_z": back_x * 2 + 1 - zh,
        "far": (x + 2) % 4 * 2 + zh, "far_z": (x + 2) % 4 * 2 + 1 - zh,
    }
    sends = (
        ("own", on), ("own", back), ("own", zx), ("own", sib),
        ("own_z", on), ("own_z", sib),
        ("ahead", back), ("behind_z", on), ("ahead", zx),
        ("behind", sib), ("ahead", sib), ("behind_z", sib),
        ("far", sib), ("far_z", sib), ("ahead_z", sib),
    )

    def piece_copy(w, k):
        slot = lbuf.at[w, q[sends[k][0]], core]
        return remote(slot, slot, l_send.at[w, k], l_recv.at[w, q[sends[k][0]], core], sends[k][1])

    def relay(w, arrived, numbers):
        for name in arrived:
            got(w, q[name], core)
        for k in numbers:
            piece_copy(w, k).start()

    def relay_a(w):
        relay(w, ("own",), (0, 1, 2, 3))

    def relay_b(w):
        relay(w, ("own_z",), (4, 5))

    def relay_c(w):
        relay(w, ("ahead", "behind", "behind_z"), (6, 7, 8, 9, 10, 11))

    def relay_d(w):
        relay(w, ("far", "far_z", "ahead_z"), (12, 13, 14))

    def relay_e(w):
        for i in range(8):
            got(w, i, 1 - core)

    def make_index():
        total = ktile[2] + krecv[3] + krecv[4] + krecv[5]
        rows = lax.broadcasted_iota(jnp.int32, (100, B), 0)
        owner = lax.broadcasted_iota(jnp.int32, (8, B), 1) // 16
        crecv[g] = ctile[...]
        rights = []
        for s in range(1, WL):
            slots = jnp.broadcast_to(pat[:, s : s + 1], (100, B))
            parts = [
                jnp.sum(jnp.where(rows == total[w : w + 1, :], slots, 0), axis=0, keepdims=True)
                for w in range(W)
            ]
            rights.append(jnp.concatenate(parts + [jnp.zeros((8 - W, B), jnp.int32)], axis=0))
        for m in range(WL):
            cols = jnp.zeros((8, B), jnp.int32)
            for t in range(8):
                cols = jnp.where(owner == t, jnp.broadcast_to(crecv[t, :, m : m + 1], (8, B)), cols)
            idx = total * WL
            for s in range(1, WL):
                idx = idx + jnp.where(rights[s - 1] == cols, s, 0)
            idxv[m] = idx
        copy = pltpu.make_async_copy(idxv, idxs, i_sem)
        copy.start()
        copy.wait()

    def product(w, gs):
        at = [place(gs, p) for p in range(2)]
        lc = jnp.concatenate(
            [lbuf[w, at[p], p, s] for p in range(2) for s in range(WL)], axis=1
        )

        def block(m, l):
            return rbuf[idxs[m, w, gs * 16 + l]]

        rc = jnp.concatenate(
            [jnp.concatenate([block(m, l) for m in range(WL)], axis=1) for l in range(2 * WL)], axis=0
        )
        return jnp.dot(lc, rc, preferred_element_type=F32)

    def p_copy(w, k, d):
        return remote(psend.at[w, k], precv.at[w, k], p_send.at[w, k], p_recv.at[w, k], d)

    def y_dev(t):
        return dev(x, (y + 1 + 2 * t) % 4, zh, zl, core)

    zl_dev = dev(x, y, zh, 1 - zl, core)

    def pair(step):
        def body(t, carry):
            step(t)
            return carry

        lax.fori_loop(0, 2, body, 0)

    def far_rows(w):
        def step(t):
            encode(psend.at[w, t], product(w, ((y + 2) % 4) * 2 + t))
            p_copy(w, t, y_dev(t)).start()

        pair(step)

    def near_rows(w):
        def step(t):
            encode(psend.at[w, 2 + t], product(w, ((y + 1 + 2 * t) % 4) * 2 + 1 - t))
            p_copy(w, 2 + t, y_dev(t)).start()

        pair(step)

    def own_rows(w):
        def step(t):
            acc[w % 3, t] = product(w, y * 2 + t)

        pair(step)

    def joined_rows(w):
        def step(t):
            p = product(w, ((y + 1 + 2 * t) % 4) * 2 + t)
            p_copy(w, t, y_dev(t)).wait_recv()
            encode(psend.at[w, 4 + t], p + decode(precv.at[w, t]))
            p_copy(w, 4 + t, y_dev(t)).start()

        pair(step)

    def plane_sum(w, tz):
        a, b = 4 - 2 * tz, 3 + 2 * tz
        p_copy(w, b, zl_dev).wait_recv()
        p_copy(w, a, zl_dev).wait_recv()
        return acc[w % 3, tz] + decode(precv.at[w, a]) + decode(precv.at[w, b])

    def cross(w):
        encode(psend.at[w, 6], plane_sum(w, 1 - zl))
        p_copy(w, 6, zl_dev).start()

    def finish(w):
        own_copy(w).wait()
        s = plane_sum(w, zl)
        p_copy(w, 6, zl_dev).wait_recv()
        s = s + decode(precv.at[w, 6])
        plain = flag_ref[g * WL + w] == 1
        c_s = jnp.where(plain, 1.0, -1.0)
        c_o = jnp.where(plain, 0.0, 2.0)
        for m in range(WL):
            o = sbuf[w, m].astype(F32)
            out[w, m] = (
                c_s * s[:, m * B : (m + 1) * B] + c_o * o
            ).astype(BF16)

    k_start()
    t_start(0)
    for o in range(1, 8):
        c_copy(o).start()
    r_copy.start()
    k_got(0)
    k_copy(krecv.at[0], 1, sib).start()
    t_start(1)
    relay_a(0)
    t_start(2)
    k_got(1)
    ktile[1] = krecv[0] + krecv[1]
    k_copy(ktile.at[1], 2, zx).start()
    relay_b(0)
    k_got(2)
    ktile[2] = ktile[1] + krecv[2]
    k_copy(ktile.at[2], 3, xpd).start()
    k_copy(ktile.at[2], 4, xmd).start()
    relay_a(1)
    relay_c(0)
    t_start(3)
    k_got(3)
    k_got(4)
    k_copy(krecv.at[3], 5, xpd).start()
    relay_b(1)
    t_start(4)
    relay_d(0)
    relay_a(2)
    for w in range(W):
        own_copy(w).start()
    for o in range(1, 8):
        remote(
            ctile, crecv.at[(g + o) % 8], c_send.at[o - 1], c_recv.at[(g + o) % 8], sib
        ).wait_recv()
    k_got(5)
    make_index()
    relay_b(2)
    r_copy.wait()

    def wave(w, carry):
        def guard(cond, f, v):
            @pl.when(cond)
            def _():
                f(v)

        def first(v):
            relay_e(v)
            far_rows(v)

        guard(w < W, first, w)
        guard(w < W - 1, relay_c, w + 1)
        guard(w < W, own_rows, w)
        guard(w < W, near_rows, w)
        guard(w < W - 3, relay_a, w + 3)
        guard(w < W - 3, relay_b, w + 3)
        guard(w < W - 1, relay_d, w + 1)
        guard(jnp.logical_and(w > 0, w < W + 1), cross, w - 1)
        guard(w < W, joined_rows, w)
        guard(w > 1, finish, w - 2)
        return carry

    lax.fori_loop(0, W + 2, wave, 0)

    def drain(w, carry):
        @pl.when(away)
        def _():
            t_copy(w).wait_send()

        for k in range(15):
            piece_copy(w, k).wait_send()
        for k in range(7):
            p_copy(w, k, zl_dev).wait_send()
        return carry

    lax.fori_loop(0, W, drain, 0)
    for o in range(1, 8):
        c_copy(o).wait_send()

    @pl.when(away)
    def _():
        k_copy(ktile.at[0], 0, t_to).wait_send()

    for k in range(1, 6):
        k_copy(ktile.at[0], k, sib).wait_send()


def body(values, pattern, branch_flag):
    vmem = pl.BlockSpec(memory_space=pltpu.VMEM)
    dma = pltpu.SemaphoreType.DMA
    return pl.pallas_call(
        kernel,
        out_shape=jax.ShapeDtypeStruct((W, WL, B, B), BF16),
        in_specs=[pl.BlockSpec(memory_space=pltpu.SMEM), pl.BlockSpec(memory_space=pl.ANY), vmem],
        out_specs=vmem,
        scratch_shapes=[
            pltpu.VMEM((500, B, B), BF16),
            pltpu.VMEM((W, WL, B, B), BF16),
            pltpu.VMEM((W, 8, 2, WL, B, B), BF16),
            pltpu.VMEM((W, 7, PR, B), jnp.int16),
            pltpu.VMEM((W, 7, PR, B), jnp.int16),
            pltpu.VMEM((8, B), jnp.int32),
            pltpu.VMEM((8, 8, B), jnp.int32),
            pltpu.VMEM((3, 8, B), jnp.int32),
            pltpu.VMEM((6, 8, B), jnp.int32),
            pltpu.VMEM((3, 2, B, R), F32),
            pltpu.VMEM((WL, 8, B), jnp.int32),
            pltpu.SMEM((WL, 8, B), jnp.int32),
            dma((W,)), dma, dma((W,)), dma((W, 15)), dma((W, 8, 2)), dma((W, 7)), dma((W, 7)),
            dma((7,)), dma((8,)), dma((6,)), dma((6,)), dma,
        ],
        compiler_params=pltpu.CompilerParams(
            collective_id=0, has_side_effects=True, vmem_limit_bytes=58 * 2**20
        ),
        cost_estimate=pl.CostEstimate(flops=8_400_000_000, bytes_accessed=20_000_000, transcendentals=0),
    )(branch_flag, values.reshape(500, B, B), pattern)


def solution(mesh):
    in_specs = (P(("row", "depth"), "col", None, None), P(("row", "depth"), "col"), P())
    out_specs = P(("row", "depth"), "col", None, None)
    return jax.shard_map(body, mesh=mesh, in_specs=in_specs, out_specs=out_specs, check_vma=False)
```
